256 devices in a mesh: row: 32 (over y, x, core), col: 8 (over z).
Axes of the slice: x: 4, y: 4, z: 8, core: 2. Of those that a mesh axis runs over, the one named last changes fastest.
Arguments:
- a_tiles: bfloat16 [32, 2048, 128, 128], P('row', 'col'), may hold values from -1.25 to 1.25
- a_rows: int32 [32, 2048], P('row', 'col'), may hold values from 0 to 47
- a_cols: int32 [32, 2048], P('row', 'col'), may hold values from 0 to 47
- a_count: int32 [32, 8], P('row', 'col'), may hold values from 64 to 256, as said below
- p_panels: bfloat16 [4096, 128, 256], P(('row', 'col')), may hold values from -1.25 to 1.25
Outputs:
- coarse_bands: float32 [8, 256, 768], P('col', 'row')
The draws below stay inside these ranges and needn't reach their ends.
Inputs may be any that keep to these rules, and one draw needn't show every extreme that they name: Only the first a_count slots of a device are live; the count reaches 256 on some devices in every draw.
All inputs are finite; a program needn't handle non-finite values.
Results may differ from the reference program's by a relative error of at most 0.0029.
Values may be sent and summed in bfloat16 or wider, within the bound.
No kernel may reach another device: no remote copies, remote signals or barrier semaphores. Data moves between devices by JAX's collectives and lax.ppermute only.
A program may use at most 64 MiB of HBM per device.

```python
import jax
import jax.numpy as jnp
from jax import lax

TILE = 128
CB = 2
PD = 16
KA = 256
NBF = 4096
N_ROW = 32
N_COL = 8


def draw_a_count(key, part):
    key = jax.random.fold_in(key, 5)
    first_key, second_key = jax.random.split(key)
    base = jax.random.randint(first_key, (N_ROW * N_COL,), KA // 4, KA // 2 + 1)
    order = jax.random.permutation(second_key, N_ROW * N_COL)
    refined = order < max(N_ROW * N_COL // 8, 1)
    return jnp.where(refined, KA, base).reshape(N_ROW, N_COL).astype(jnp.int32)


def place_ends(values, own_key, smallest, high):
    longest = values.shape.index(max(values.shape))
    spots = []
    for shift in (0, 1):
        where = [jax.random.randint(jax.random.fold_in(own_key, axis), (), 0, length) for axis, length in enumerate(values.shape)]
        where[longest] = (where[longest] + shift) % values.shape[longest]
        spots.append(tuple(where))
    return values.at[spots[0]].set(smallest).at[spots[1]].set(high)


def shard_levels(rng, extent, pieces, smallest, top_value):
    loudness, own = 1.0, jax.random.fold_in(rng, 6)
    for position, shards_of in pieces:
        heights = jnp.exp(jax.random.uniform(jax.random.fold_in(own, position), (shards_of,), jnp.float32, smallest / len(pieces), top_value / len(pieces)))
        loudness = loudness * jnp.repeat(heights, extent[position] // shards_of).reshape([-1 if axis == position else 1 for axis in range(len(extent))])
    return loudness


def scatter_about(key, extent, width, limit, cuts=(), kind=jnp.bfloat16):
    loudness = shard_levels(key, extent, cuts, -0.22, 0.18) if cuts else 1.0
    values = jax.random.normal(key, extent, jnp.float32) * width * loudness
    return jnp.minimum(jnp.maximum(values, -limit), limit).astype(kind)


def setup_inputs(seed: int = 0) -> dict:
    streams_of = jax.random.split(jax.random.key(seed), 6)
    a_tiles = scatter_about(streams_of[0], (N_ROW, N_COL * KA, TILE, TILE), (TILE ** -0.5), 1.25, ((0, 32), (1, 8)))
    a_rows = place_ends(jax.random.randint(streams_of[1], (N_ROW, N_COL * KA), 0, 3 * PD), jax.random.fold_in(streams_of[1], 1), 0, (3 * PD) - 1).astype(jnp.int32)
    a_cols = place_ends(jax.random.randint(streams_of[2], (N_ROW, N_COL * KA), 0, 3 * PD), jax.random.fold_in(streams_of[2], 1), 0, (3 * PD) - 1).astype(jnp.int32)
    a_count = draw_a_count(jax.random.fold_in(streams_of[5], 71), 0)
    p_panels = scatter_about(streams_of[4], (NBF, TILE, CB * TILE), (TILE ** -0.5), 1.25, ((0, 256),))
    return {"a_tiles": a_tiles, "a_rows": a_rows, "a_cols": a_cols, "a_count": a_count, "p_panels": p_panels}


def reference(a_tiles, a_rows, a_cols, a_count, p_panels):
    band_width = CB * TILE
    grid = p_panels.reshape(N_ROW, N_COL, PD, TILE, band_width)
    padded = jnp.pad(grid, ((0, 0), (1, 1), (0, 0), (0, 0), (0, 0)))
    padded_rows = jnp.pad(grid, ((1, 1), (0, 0), (0, 0), (0, 0), (0, 0)))
    result = jnp.zeros((N_COL + 2, band_width, 3 * band_width), jnp.float32)

    def device_term(result, flat):
        mesh_row = (flat // N_COL).astype(jnp.int32)
        mesh_col = (flat % N_COL).astype(jnp.int32)
        col_block = lax.dynamic_index_in_dim(padded_rows, mesh_col, 1, False)
        col_side = lax.dynamic_slice_in_dim(col_block, mesh_row, 3, 0).reshape(3 * PD, TILE, band_width)
        row_block = lax.dynamic_index_in_dim(padded, mesh_row, 0, False)
        row_side = lax.dynamic_slice_in_dim(row_block, mesh_col, 3, 0).reshape(3 * PD, TILE, band_width)
        first = (mesh_col * KA).astype(jnp.int32)
        tiles = lax.dynamic_slice_in_dim(lax.dynamic_index_in_dim(a_tiles, mesh_row, 0, False), first, KA, 0)
        row_ids = lax.dynamic_slice_in_dim(lax.dynamic_index_in_dim(a_rows, mesh_row, 0, False), first, KA, 0)
        col_ids = lax.dynamic_slice_in_dim(lax.dynamic_index_in_dim(a_cols, mesh_row, 0, False), first, KA, 0)
        live_count = a_count[mesh_row, mesh_col]
        right_panels = col_side[col_ids].astype(jnp.float32)
        applied = jnp.einsum("tab,tbw->taw", tiles.astype(jnp.float32), right_panels).astype(jnp.bfloat16)
        left_panels = row_side[row_ids].astype(jnp.float32)
        contribution = jnp.einsum("tkm,tkn->tmn", left_panels, applied.astype(jnp.float32))
        in_use = jnp.arange(KA) < live_count
        band_offset = row_ids // PD
        selector = ((band_offset[:, None] == jnp.arange(3)[None, :]) & in_use[:, None]).astype(jnp.float32)
        partial_value = jnp.einsum("to,tmn->omn", selector, contribution, precision=lax.Precision.HIGHEST)
        result = result.at[mesh_col + 2, :, 0:band_width].add(partial_value[2])
        result = result.at[mesh_col + 1, :, band_width:2 * band_width].add(partial_value[1])
        result = result.at[mesh_col, :, 2 * band_width:3 * band_width].add(partial_value[0])
        return result, None

    result, _ = lax.scan(device_term, result, jnp.arange(N_ROW * N_COL, dtype=jnp.int32))
    return result[1:N_COL + 1]
```

```python
import functools

import jax
import jax.numpy as jnp
from jax import lax
from jax.experimental import pallas as pl
from jax.experimental.pallas import tpu as pltpu
from jax.sharding import PartitionSpec as P

BF = jnp.bfloat16
F32 = jnp.float32
PANELS = 16
TILE = 128
BAND = 256
SLOTS = 256
UNROLL = 8
RING = 4
LIST = SLOTS + UNROLL
ANY = pl.BlockSpec(memory_space=pl.ANY)
SM = pl.BlockSpec(memory_space=pltpu.SMEM)
VM = pl.BlockSpec(memory_space=pltpu.VMEM)
X, Y = 4, 4


def vmem(mib):
    return pltpu.CompilerParams(vmem_limit_bytes=mib * 2**20)


def cost(flops, nbytes):
    return pl.CostEstimate(flops=flops, bytes_accessed=nbytes, transcendentals=0)


def plan_kernel(core, rows, cols, count, codes, counts):
    partner = jnp.where(core[0] == 0, 2, 0)

    def put(t, pos):
        n0, n1 = pos
        r, c = rows[0, t], cols[0, t]
        q = lax.div(c, PANELS)
        k = c - q * PANELS
        first = (q == 1) | (q == partner)
        at = jnp.where(first, n0, LIST + n1)
        codes[at] = t * 4096 + r * 64 + jnp.where(q == partner, k + PANELS, k)
        return jnp.where(first, n0 + 1, n0), jnp.where(first, n1, n1 + 1)

    n0, n1 = lax.fori_loop(0, count[0, 0], put, (jnp.int32(0), jnp.int32(0)))
    counts[0] = n0
    counts[1] = n1
    for i in range(UNROLL):
        codes[n0 + i] = 3 * PANELS * 64
        codes[LIST + n1 + i] = 3 * PANELS * 64


def plan(core, rows, cols, count):
    return pl.pallas_call(
        plan_kernel,
        out_shape=(
            jax.ShapeDtypeStruct((2 * LIST,), jnp.int32),
            jax.ShapeDtypeStruct((2,), jnp.int32),
        ),
        in_specs=[SM] * 4,
        out_specs=(SM, SM),
        name="plan",
        cost_estimate=cost(10**9, 10**4),
    )(core, rows, cols, count)


def apply_tiles(which, codes, counts, a_hbm, panels, sums, cbuf, abuf, csem, asem, prepare):
    base = which * LIST
    groups = lax.div(counts[which] + UNROLL - 1, UNROLL)
    loads = [
        pltpu.make_async_copy(p, cbuf.at[pl.ds(PANELS * i, PANELS)], csem.at[i])
        for i, p in enumerate(panels)
    ]
    for load in loads:
        load.start()

    def fetch(g):
        place = lax.rem(g, RING) * UNROLL
        for u in range(UNROLL):
            t = lax.div(codes[base + g * UNROLL + u], 4096)
            pltpu.make_async_copy(a_hbm.at[0, t], abuf.at[place + u], asem.at[place + u]).start()

    for g in range(RING - 1):
        @pl.when(g < groups)
        def _():
            fetch(g)

    prepare()
    for load in loads:
        load.wait()

    def step(g, carry):
        @pl.when(g + RING - 1 < groups)
        def _():
            fetch(g + RING - 1)

        place = lax.rem(g, RING) * UNROLL
        for u in range(UNROLL):
            pltpu.make_async_copy(a_hbm.at[0, 0], abuf.at[place + u], asem.at[place + u]).wait()
        applied, rows = [], []
        for u in range(UNROLL):
            code = codes[base + g * UNROLL + u]
            rows.append(lax.rem(lax.div(code, 64), 64))
            product = jnp.dot(
                abuf[place + u], cbuf[lax.rem(code, 64)], preferred_element_type=F32
            )
            applied.append(product.astype(BF).astype(F32))
        for u in range(UNROLL):
            sums[rows[u]] += applied[u]
        return carry

    lax.fori_loop(0, groups, step, 0)


def first_kernel(codes, counts, a_hbm, own, partner, sums, cbuf, abuf, csem, asem):
    def clear():
        def zero(i, carry):
            sums[i] = jnp.zeros((TILE, BAND), F32)
            return carry

        lax.fori_loop(0, 3 * PANELS + 1, zero, 0)

    apply_tiles(0, codes, counts, a_hbm, (own, partner), sums, cbuf, abuf, csem, asem, clear)


def second_kernel(codes, counts, a_hbm, other, before, turned, sums, cbuf, abuf, csem, asem, ssem):
    def load_sums():
        copy = pltpu.make_async_copy(before, sums, ssem)
        copy.start()
        copy.wait()

    apply_tiles(1, codes, counts, a_hbm, (other,), sums, cbuf, abuf, csem, asem, load_sums)
    for k in range(3 * PANELS):
        lanes = pl.ds((k % PANELS) * TILE, TILE)
        turned[k // PANELS, :, lanes] = sums[k].T.astype(BF)


SUMS = (3 * PANELS + 1, TILE, BAND)


def scratch(panel_sets):
    return [
        pltpu.VMEM((panel_sets * PANELS, TILE, BAND), BF),
        pltpu.VMEM((RING * UNROLL, TILE, TILE), BF),
        pltpu.SemaphoreType.DMA((panel_sets,)),
        pltpu.SemaphoreType.DMA((RING * UNROLL,)),
    ]


def first_sums(codes, counts, a_tiles, own, partner):
    return pl.pallas_call(
        first_kernel,
        out_shape=jax.ShapeDtypeStruct(SUMS, F32),
        in_specs=[SM, SM, ANY, ANY, ANY],
        out_specs=VM,
        scratch_shapes=scratch(2),
        compiler_params=vmem(24),
        name="first_sums",
        cost_estimate=cost(10 * 10**9, 16 * 2**20),
    )(codes, counts, a_tiles, own, partner)


def second_sums(codes, counts, a_tiles, other, before):
    return pl.pallas_call(
        second_kernel,
        out_shape=jax.ShapeDtypeStruct((3, BAND, PANELS * TILE), BF),
        in_specs=[SM, SM, ANY, ANY, ANY],
        out_specs=VM,
        scratch_shapes=[pltpu.VMEM(SUMS, F32)] + scratch(1) + [pltpu.SemaphoreType.DMA],
        compiler_params=vmem(24),
        name="second_sums",
        cost_estimate=cost(10 * 10**9, 16 * 2**20),
    )(codes, counts, a_tiles, other, before)


def couple_kernel(core, turned, low, own, high, out):
    me = core[0]
    for o, panels in enumerate((low, own, high)):
        rows = panels[...].reshape(PANELS * TILE, BAND)
        term = jnp.dot(turned[o], rows, preferred_element_type=F32).T
        lanes = pl.ds(o * BAND, BAND)
        for block in range(BAND // 8):
            y, x, c = block // (2 * X), (block // 2) % X, block % 2
            out[me ^ c, x, y, :, lanes] = term[block * 8:(block + 1) * 8]


def couple(core, turned, low, own, high):
    return pl.pallas_call(
        couple_kernel,
        out_shape=jax.ShapeDtypeStruct((2, X, Y, 8, 3 * BAND), F32),
        in_specs=[SM, VM, VM, VM, VM],
        out_specs=VM,
        compiler_params=vmem(24),
        name="couple",
        cost_estimate=cost(10**9, 6 * 2**20),
    )(core, turned, low, own, high)


def shift(value, axis, pairs):
    return lax.ppermute(value, axis, pairs)


def exchange_sum(value, place, pairs_of, kind):
    total = lax.dynamic_index_in_dim(value, place, 0, False)
    for k in range(1, value.shape[0]):
        there = lax.rem(place + k, value.shape[0])
        block = lax.dynamic_index_in_dim(value, there, 0, False).astype(kind)
        total = total + shift(block, "row", pairs_of(k)).astype(F32)
    return total


def at(y, x, core):
    return (y % Y * X + x % X) * 2 + core


PLACES = [(y, x, c) for y in range(Y) for x in range(X) for c in range(2)]


def along_x(k):
    return [(at(y, x, c), at(y, x + k, c)) for y, x, c in PLACES]


def along_y(k):
    return [(at(y, x, c), at(y + k, x, c)) for y, x, c in PLACES]


def local(a_tiles, a_rows, a_cols, a_count, p_panels):
    n_row, n_col = lax.axis_size("row"), lax.axis_size("col")
    row = lax.axis_index("row")
    core, x, y = row % 2, row // 2 % X, row // (2 * X)
    up = [(i, i + 1) for i in range(n_col - 1)]
    down = [(j, i) for i, j in up]
    pairs = [(i, i ^ 1) for i in range(n_row)]
    bridges = [(i, i + 1) for i in range(1, n_row - 1, 2)]
    bridges += [(j, i) for i, j in bridges]
    low = shift(p_panels, "col", up)
    high = shift(p_panels, "col", down)
    other = shift(p_panels, "row", bridges)
    partner = shift(p_panels, "row", pairs)
    core_id = core.astype(jnp.int32)[None]
    codes, counts = plan(core_id, a_rows, a_cols, a_count)
    before = first_sums(codes, counts, a_tiles, p_panels, partner)
    turned = second_sums(codes, counts, a_tiles, other, before)
    terms = couple(core_id, turned, low, p_panels, high)
    chip = terms[0] + shift(terms[1], "row", pairs)
    line = exchange_sum(chip.reshape(X, Y * 8, 3 * BAND), x, along_x, BF)
    rows = exchange_sum(line.reshape(Y, 8, 3 * BAND), y, along_y, F32)
    from_lower = shift(rows[:, 2 * BAND:], "col", up)
    from_upper = shift(rows[:, :BAND], "col", down)
    return jnp.concatenate([from_lower, rows[:, BAND:2 * BAND], from_upper], axis=1)[None]


def solution(mesh):
    in_specs = (
        P("row", "col", None, None),
        P("row", "col"),
        P("row", "col"),
        P("row", "col"),
        P(("row", "col"), None, None),
    )
    out_specs = P("col", "row", None)
    return jax.shard_map(local, mesh=mesh, in_specs=in_specs, out_specs=out_specs, check_vma=False)
```

```python
import functools

import jax
import jax.numpy as jnp
from jax import lax
from jax.experimental import pallas as pl
from jax.experimental.pallas import tpu as pltpu
from jax.sharding import PartitionSpec as P

BF = jnp.bfloat16
F32 = jnp.float32
PANELS = 16
TILE = 128
BAND = 256
SLOTS = 256
UNROLL = 16
STEP = 8
LIST = SLOTS + UNROLL
SM = pl.BlockSpec(memory_space=pltpu.SMEM)
VM = pl.BlockSpec(memory_space=pltpu.VMEM)
SUMS = (3 * PANELS + 1, TILE, BAND)
X, Y = 4, 4
TERMS = (2, X, Y, 3, 8, BAND)


def vmem(mib):
    return pltpu.CompilerParams(vmem_limit_bytes=mib * 2**20)


def cost(flops, nbytes):
    return pl.CostEstimate(flops=flops, bytes_accessed=nbytes, transcendentals=0)


def plan_kernel(rows, cols, count, codes, counts):
    live = count[0, 0]

    def put(step, pos):
        n = list(pos)
        for u in range(STEP):
            t = step * STEP + u
            r, c = rows[0, t], cols[0, t]
            q = c >> 4
            base = jnp.where(q == 0, n[0], jnp.where(q == 1, n[1], n[2]))
            ok = t < live
            codes[jnp.where(ok, base, 3 * LIST)] = t * 1024 + r * 16 + (c & 15)
            n = [n[i] + (ok & (q == i)).astype(jnp.int32) for i in range(3)]
        return tuple(n)

    steps = (live + STEP - 1) // STEP
    ends = lax.fori_loop(0, steps, put, tuple(jnp.int32(i * LIST) for i in range(3)))
    for i in range(3):
        counts[i] = ends[i] - i * LIST
        for u in range(UNROLL):
            codes[ends[i] + u] = 3 * PANELS * 16


def plan(rows, cols, count):
    return pl.pallas_call(
        plan_kernel,
        out_shape=(
            jax.ShapeDtypeStruct((3 * LIST + 1,), jnp.int32),
            jax.ShapeDtypeStruct((3,), jnp.int32),
        ),
        in_specs=[SM] * 3,
        out_specs=(SM, SM),
        compiler_params=vmem(2),
        name="plan",
        cost_estimate=cost(30 * 10**9, 10**4),
    )(rows, cols, count)


def apply_tiles(which, codes, counts, a_tiles, panels, sums):
    def step(g, carry):
        applied, rows = [], []
        for u in range(UNROLL):
            code = codes[which * LIST + g * UNROLL + u]
            rows.append((code >> 4) & 63)
            product = jnp.dot(a_tiles[0, code >> 10], panels[code & 15], preferred_element_type=F32)
            applied.append(product.astype(BF).astype(F32))
        for u in range(UNROLL):
            sums[rows[u]] += applied[u]
        return carry

    lax.fori_loop(0, (counts[which] + UNROLL - 1) // UNROLL, step, 0)


def first_kernel(place, codes, counts, a_tiles, own, partner, sums):
    def zero(i, carry):
        sums[i] = jnp.zeros((TILE, BAND), F32)
        return carry

    lax.fori_loop(0, 3 * PANELS + 1, zero, 0)
    apply_tiles(1, codes, counts, a_tiles, own, sums)
    apply_tiles(2 - 2 * (place[0] & 1), codes, counts, a_tiles, partner, sums)


def put_term(row, turned, panels, slot, terms):
    term = jnp.dot(turned, panels[...].reshape(PANELS * TILE, BAND), preferred_element_type=F32).T
    for block in range(BAND // 8):
        to = row ^ block
        terms[to & 1, (to >> 1) & 3, to >> 3, slot] = term[block * 8:(block + 1) * 8]


def second_kernel(place, codes, counts, a_tiles, other, before, own, sums, turned, terms):
    apply_tiles(2 * (place[0] & 1), codes, counts, a_tiles, other, sums)
    for k in range(3 * PANELS):
        lanes = pl.ds((k % PANELS) * TILE, TILE)
        turned[k // PANELS, :, lanes] = sums[k].astype(BF).T
    put_term(place[0], turned[1], own, 1, terms)


def first_sums(place, codes, counts, a_tiles, own, partner):
    return pl.pallas_call(
        first_kernel,
        out_shape=jax.ShapeDtypeStruct(SUMS, F32),
        in_specs=[SM] * 3 + [VM] * 3,
        out_specs=VM,
        compiler_params=vmem(20),
        name="first_sums",
        cost_estimate=cost(10 * 10**9, 16 * 2**20),
    )(place, codes, counts, a_tiles, own, partner)


def second_sums(place, codes, counts, a_tiles, other, before, own):
    return pl.pallas_call(
        second_kernel,
        out_shape=(
            jax.ShapeDtypeStruct(SUMS, F32),
            jax.ShapeDtypeStruct((3, BAND, PANELS * TILE), BF),
            jax.ShapeDtypeStruct(TERMS, F32),
        ),
        in_specs=[SM] * 3 + [VM] * 4,
        out_specs=(VM, VM, VM),
        input_output_aliases={5: 0},
        compiler_params=vmem(24),
        name="second_sums",
        cost_estimate=cost(10 * 10**9, 16 * 2**20),
    )(place, codes, counts, a_tiles, other, before, own)[1:]


def couple_kernel(place, turned, even, odd, before, terms):
    even_offset = place[1]
    put_term(place[0], turned[even_offset], even, 0, terms)
    put_term(place[0], turned[2 - even_offset], odd, 2, terms)


def couple(place, turned, even, odd, before):
    return pl.pallas_call(
        couple_kernel,
        out_shape=jax.ShapeDtypeStruct(TERMS, F32),
        in_specs=[SM] + [VM] * 4,
        out_specs=VM,
        input_output_aliases={4: 0},
        compiler_params=vmem(12),
        name="couple",
        cost_estimate=cost(10**9, 6 * 2**20),
    )(place, turned, even, odd, before)


def swap_sum(value, shift, kind):
    total = value[0]
    for i in range(1, value.shape[0]):
        pairs = [(r, r ^ (i << shift)) for r in range(2 * X * Y)]
        total = total + lax.ppermute(value[i].astype(kind), "row", pairs).astype(F32)
    return total


def both_ways(pairs):
    return pairs + [(j, i) for i, j in pairs]


def local(a_tiles, a_rows, a_cols, a_count, p_panels):
    n_row, n_col = lax.axis_size("row"), lax.axis_size("col")
    row, col = lax.axis_index("row"), lax.axis_index("col")
    even_pairs = both_ways([(i, i + 1) for i in range(0, n_col - 1, 2)])
    odd_pairs = both_ways([(i, i + 1) for i in range(1, n_col - 1, 2)])
    chip = both_ways([(i, i + 1) for i in range(0, n_row - 1, 2)])
    bridges = both_ways([(i, i + 1) for i in range(1, n_row - 1, 2)])
    even = lax.ppermute(p_panels, "col", even_pairs)
    odd = lax.ppermute(p_panels, "col", odd_pairs)
    other = lax.ppermute(p_panels, "row", bridges)
    partner = lax.ppermute(p_panels, "row", chip)
    low_col = (col & 1) == 0
    place = jnp.stack([row, jnp.where(low_col, 2, 0)]).astype(jnp.int32)
    codes, counts = plan(a_rows, a_cols, a_count)
    before = first_sums(place, codes, counts, a_tiles, p_panels, partner)
    turned, terms = second_sums(place, codes, counts, a_tiles, other, before, p_panels)
    terms = couple(place, turned, even, odd, terms)
    terms = swap_sum(terms, 0, F32)
    terms = swap_sum(terms, 1, BF)
    terms = swap_sum(terms, 3, F32)
    from_even = lax.ppermute(terms[0], "col", even_pairs)
    from_odd = lax.ppermute(terms[2], "col", odd_pairs)
    lower = jnp.where(low_col, from_odd, from_even)
    upper = jnp.where(low_col, from_even, from_odd)
    return jnp.concatenate([lower, terms[1], upper], axis=1)[None]


def solution(mesh):
    in_specs = (
        P("row", "col", None, None),
        P("row", "col"),
        P("row", "col"),
        P("row", "col"),
        P(("row", "col"), None, None),
    )
    out_specs = P("col", "row", None)
    return jax.shard_map(local, mesh=mesh, in_specs=in_specs, out_specs=out_specs, check_vma=False)
```

```python
import functools

import jax
import jax.numpy as jnp
from jax import lax
from jax.experimental import pallas as pl
from jax.experimental.pallas import tpu as pltpu
from jax.sharding import PartitionSpec as P

BF = jnp.bfloat16
F32 = jnp.float32
PANELS = 16
TILE = 128
BAND = 256
SLOTS = 256
UNROLL = 16
STEP = 8
LIST = SLOTS + UNROLL
SM = pl.BlockSpec(memory_space=pltpu.SMEM)
VM = pl.BlockSpec(memory_space=pltpu.VMEM)
SUMS = (3 * PANELS + 1, TILE, BAND)
CHIPS = 16
TERMS = (2, CHIPS, 3, 8, BAND)


def vmem(mib):
    return pltpu.CompilerParams(vmem_limit_bytes=mib * 2**20)


def cost(flops, nbytes):
    return pl.CostEstimate(flops=flops, bytes_accessed=nbytes, transcendentals=0)


def plan_kernel(rows, cols, count, codes, counts):
    live = count[0, 0]

    def put(step, pos):
        n = list(pos)
        for u in range(STEP):
            t = step * STEP + u
            r, c = rows[0, t], cols[0, t]
            q = c >> 4
            base = jnp.where(q == 0, n[0], jnp.where(q == 1, n[1], n[2]))
            ok = t < live
            codes[jnp.where(ok, base, 3 * LIST)] = t * 1024 + r * 16 + (c & 15)
            n = [n[i] + (ok & (q == i)).astype(jnp.int32) for i in range(3)]
        return tuple(n)

    steps = (live + STEP - 1) // STEP
    ends = lax.fori_loop(0, steps, put, tuple(jnp.int32(i * LIST) for i in range(3)))
    for i in range(3):
        counts[i] = ends[i] - i * LIST
        for u in range(UNROLL):
            codes[ends[i] + u] = 3 * PANELS * 16


def plan(rows, cols, count):
    return pl.pallas_call(
        plan_kernel,
        out_shape=(
            jax.ShapeDtypeStruct((3 * LIST + 1,), jnp.int32),
            jax.ShapeDtypeStruct((3,), jnp.int32),
        ),
        in_specs=[SM] * 3,
        out_specs=(SM, SM),
        compiler_params=vmem(2),
        name="plan",
        cost_estimate=cost(30 * 10**9, 10**4),
    )(rows, cols, count)


def apply_tiles(which, codes, counts, a_tiles, panels, sums):
    def step(g, carry):
        applied, rows = [], []
        for u in range(UNROLL):
            code = codes[which * LIST + g * UNROLL + u]
            rows.append((code >> 4) & 63)
            product = jnp.dot(a_tiles[0, code >> 10], panels[code & 15], preferred_element_type=F32)
            applied.append(product.astype(BF).astype(F32))
        for u in range(UNROLL):
            sums[rows[u]] += applied[u]
        return carry

    lax.fori_loop(0, (counts[which] + UNROLL - 1) // UNROLL, step, 0)


def first_kernel(codes, counts, a_tiles, own, partner, sums):
    def zero(i, carry):
        sums[i] = jnp.zeros((TILE, BAND), F32)
        return carry

    lax.fori_loop(0, 3 * PANELS + 1, zero, 0)
    apply_tiles(1, codes, counts, a_tiles, own, sums)
    apply_tiles(2 - 2 * (lax.axis_index("row") & 1), codes, counts, a_tiles, partner, sums)


def put_term(turned, panels, slot, terms):
    here = lax.axis_index("row") & 1
    term = jnp.dot(turned, panels[...].reshape(PANELS * TILE, BAND), preferred_element_type=F32).T
    for block in range(BAND // 8):
        core = (0, block & 1, 1)[slot]
        unit = 2 if slot == 1 else block & 1
        terms[here ^ core, block >> 1, unit] = term[block * 8:(block + 1) * 8]


def second_kernel(codes, counts, a_tiles, other, before, own, sums, turned, terms):
    apply_tiles(2 * (lax.axis_index("row") & 1), codes, counts, a_tiles, other, sums)
    for k in range(3 * PANELS):
        lanes = pl.ds((k % PANELS) * TILE, TILE)
        turned[k // PANELS, :, lanes] = sums[k].astype(BF).T
    put_term(turned[1], own, 1, terms)


def first_sums(codes, counts, a_tiles, own, partner):
    return pl.pallas_call(
        first_kernel,
        out_shape=jax.ShapeDtypeStruct(SUMS, F32),
        in_specs=[SM] * 2 + [VM] * 3,
        out_specs=VM,
        compiler_params=vmem(20),
        name="first_sums",
        cost_estimate=cost(10 * 10**9, 16 * 2**20),
    )(codes, counts, a_tiles, own, partner)


def second_sums(codes, counts, a_tiles, other, before, own):
    return pl.pallas_call(
        second_kernel,
        out_shape=(
            jax.ShapeDtypeStruct(SUMS, F32),
            jax.ShapeDtypeStruct((3, BAND, PANELS * TILE), BF),
            jax.ShapeDtypeStruct(TERMS, F32),
        ),
        in_specs=[SM] * 2 + [VM] * 4,
        out_specs=(VM, VM, VM),
        input_output_aliases={4: 0},
        compiler_params=vmem(24),
        name="second_sums",
        cost_estimate=cost(10 * 10**9, 16 * 2**20),
    )(codes, counts, a_tiles, other, before, own)[1:]


def couple_kernel(turned, panels, before, terms, *, slot):
    next_band = 2 - 2 * (lax.axis_index("col") & 1)
    put_term(turned[next_band if slot == 0 else 2 - next_band], panels, slot, terms)


def couple(turned, panels, before, slot):
    return pl.pallas_call(
        functools.partial(couple_kernel, slot=slot),
        out_shape=jax.ShapeDtypeStruct(TERMS, F32),
        in_specs=[VM] * 3,
        out_specs=VM,
        input_output_aliases={2: 0},
        compiler_params=vmem(12),
        name="couple%d" % slot,
        cost_estimate=cost(10**9, 6 * 2**20),
    )(turned, panels, before)


def both_ways(pairs):
    return pairs + [(j, i) for i, j in pairs]


def local(a_tiles, a_rows, a_cols, a_count, p_panels):
    n_row, n_col = lax.axis_size("row"), lax.axis_size("col")
    row, col = lax.axis_index("row"), lax.axis_index("col")
    even_pairs = both_ways([(i, i + 1) for i in range(0, n_col - 1, 2)])
    odd_pairs = both_ways([(i, i + 1) for i in range(1, n_col - 1, 2)])
    chip = both_ways([(i, i + 1) for i in range(0, n_row - 1, 2)])
    bridges = both_ways([(i, i + 1) for i in range(1, n_row - 1, 2)])
    even = lax.ppermute(p_panels, "col", even_pairs)
    odd = lax.ppermute(p_panels, "col", odd_pairs)
    low_col = (col & 1) == 0
    def sums(_):
        other = lax.ppermute(p_panels, "row", bridges)
        partner = lax.ppermute(p_panels, "row", chip)
        codes, counts = plan(a_rows, a_cols, a_count)
        before = first_sums(codes, counts, a_tiles, p_panels, partner)
        turned, terms = second_sums(codes, counts, a_tiles, other, before, p_panels)
        return turned, terms

    def nothing(_):
        return jnp.zeros((3, BAND, PANELS * TILE), BF), jnp.zeros(TERMS, F32)

    turned, terms = lax.cond(row < n_row, sums, nothing, 0)
    terms = couple(turned, even, terms, 0)
    terms = couple(turned, odd, terms, 2)
    terms = terms[0] + lax.ppermute(terms[1], "row", chip)
    groups = [list(range(c, n_row, 2)) for c in range(2)]
    terms = lax.all_to_all(terms.astype(BF), "row", 0, 0, axis_index_groups=groups).astype(F32).sum(0)
    pairs = [
        (r * n_col + i, r * n_col + j)
        for r in range(n_row)
        for i, j in (odd_pairs if r & 1 else even_pairs)
    ]
    got = lax.ppermute(terms[:2], ("row", "col"), pairs)
    first_core = (row & 1) == 0
    kept = jnp.where(first_core, got[0], got[1])
    given = lax.ppermute(jnp.where(first_core, got[1], got[0]), "row", chip)
    from_even = jnp.where(first_core, kept, given)
    from_odd = jnp.where(first_core, given, kept)
    lower = jnp.where(low_col, from_odd, from_even)
    upper = jnp.where(low_col, from_even, from_odd)
    return jnp.concatenate([lower, terms[2], upper], axis=1)[None]


def solution(mesh):
    in_specs = (
        P("row", "col", None, None),
        P("row", "col"),
        P("row", "col"),
        P("row", "col"),
        P(("row", "col"), None, None),
    )
    out_specs = P("col", "row", None)
    return jax.shard_map(local, mesh=mesh, in_specs=in_specs, out_specs=out_specs, check_vma=False)
```

```python
import functools

import jax
import jax.numpy as jnp
from jax import lax
from jax.experimental import pallas as pl
from jax.experimental.pallas import tpu as pltpu
from jax.sharding import PartitionSpec as P

BF = jnp.bfloat16
F32 = jnp.float32
PANELS = 16
TILE = 128
BAND = 256
SLOTS = 256
UNROLL = 16
STEP = 8
LIST = SLOTS + UNROLL
SM = pl.BlockSpec(memory_space=pltpu.SMEM)
VM = pl.BlockSpec(memory_space=pltpu.VMEM)
SUMS = (3 * PANELS + 1, TILE, BAND)
CHIPS = 16
TERMS = (CHIPS, 16, BAND)
TURNED = (BAND, PANELS * TILE)


def vmem(mib):
    return pltpu.CompilerParams(vmem_limit_bytes=mib * 2**20)


def cost(flops, nbytes):
    return pl.CostEstimate(flops=flops, bytes_accessed=nbytes, transcendentals=0)


def plan_kernel(rows, cols, count, codes, counts):
    live = count[0, 0]

    def put(step, pos):
        n = list(pos)
        for u in range(STEP):
            t = step * STEP + u
            r, c = rows[0, t], cols[0, t]
            q = c >> 4
            base = jnp.where(q == 0, n[0], jnp.where(q == 1, n[1], n[2]))
            ok = t < live
            codes[jnp.where(ok, base, 3 * LIST)] = t * 1024 + r * 16 + (c & 15)
            n = [n[i] + (ok & (q == i)).astype(jnp.int32) for i in range(3)]
        return tuple(n)

    steps = (live + STEP - 1) // STEP
    ends = lax.fori_loop(0, steps, put, tuple(jnp.int32(i * LIST) for i in range(3)))
    for i in range(3):
        counts[i] = ends[i] - i * LIST
        for u in range(UNROLL):
            codes[ends[i] + u] = 3 * PANELS * 16


def plan(rows, cols, count):
    return pl.pallas_call(
        plan_kernel,
        out_shape=(
            jax.ShapeDtypeStruct((3 * LIST + 1,), jnp.int32),
            jax.ShapeDtypeStruct((3,), jnp.int32),
        ),
        in_specs=[SM] * 3,
        out_specs=(SM, SM),
        compiler_params=vmem(2),
        name="plan",
        cost_estimate=cost(30 * 10**9, 10**4),
    )(rows, cols, count)


def apply_tiles(which, codes, counts, a_tiles, panels, sums):
    def step(g, carry):
        applied, rows = [], []
        for u in range(UNROLL):
            code = codes[which * LIST + g * UNROLL + u]
            rows.append((code >> 4) & 63)
            product = jnp.dot(a_tiles[0, code >> 10], panels[code & 15], preferred_element_type=F32)
            applied.append(product.astype(BF).astype(F32))
        for u in range(UNROLL):
            sums[rows[u]] += applied[u]
        return carry

    lax.fori_loop(0, (counts[which] + UNROLL - 1) // UNROLL, step, 0)


def first_kernel(codes, counts, a_tiles, own, partner, sums):
    def zero(i, carry):
        sums[i] = jnp.zeros((TILE, BAND), F32)
        return carry

    lax.fori_loop(0, 3 * PANELS + 1, zero, 0)
    apply_tiles(1, codes, counts, a_tiles, own, sums)
    apply_tiles(2 - 2 * (lax.axis_index("row") & 1), codes, counts, a_tiles, partner, sums)


def term_of(turned, panels):
    rows = panels[...].reshape(PANELS * TILE, BAND)
    return jnp.dot(turned[...], rows, preferred_element_type=F32)


def by_chip(term):
    return term.T.reshape(TERMS).astype(BF)


def second_kernel(
    codes, counts, a_tiles, other, before, own, sums, mine, theirs, terms, turned
):
    core = lax.axis_index("row") & 1
    apply_tiles(2 * core, codes, counts, a_tiles, other, sums)
    offset = 2 * (1 - ((lax.axis_index("col") ^ core) & 1))
    for part, ref in ((offset, mine), (2 - offset, theirs), (1, turned)):
        for k in range(PANELS):
            ref[:, pl.ds(k * TILE, TILE)] = sums[part * PANELS + k].astype(BF).T
    terms[...] = by_chip(term_of(turned, own))


def first_sums(codes, counts, a_tiles, own, partner):
    return pl.pallas_call(
        first_kernel,
        out_shape=jax.ShapeDtypeStruct(SUMS, F32),
        in_specs=[SM] * 2 + [VM] * 3,
        out_specs=VM,
        compiler_params=vmem(20),
        name="first_sums",
        cost_estimate=cost(10 * 10**9, 16 * 2**20),
    )(codes, counts, a_tiles, own, partner)


def second_sums(codes, counts, a_tiles, other, before, own):
    return pl.pallas_call(
        second_kernel,
        out_shape=(
            jax.ShapeDtypeStruct(SUMS, F32),
            jax.ShapeDtypeStruct(TURNED, BF),
            jax.ShapeDtypeStruct(TURNED, BF),
            jax.ShapeDtypeStruct(TERMS, BF),
        ),
        in_specs=[SM] * 2 + [VM] * 4,
        out_specs=(VM, VM, VM, VM),
        scratch_shapes=[pltpu.VMEM(TURNED, BF)],
        input_output_aliases={4: 0},
        compiler_params=vmem(24),
        name="second_sums",
        cost_estimate=cost(10 * 10**9, 16 * 2**20),
    )(codes, counts, a_tiles, other, before, own)[1:]


def partner_kernel(received, cross, part):
    part[...] = term_of(received, cross)


def partner_term(received, cross):
    return pl.pallas_call(
        partner_kernel,
        out_shape=jax.ShapeDtypeStruct((BAND, BAND), F32),
        in_specs=[VM] * 2,
        out_specs=VM,
        compiler_params=vmem(8),
        name="partner_term",
        cost_estimate=cost(10**9, 6 * 2**20),
    )(received, cross)


def couple_kernel(mine, straight, part, own, out):
    upper_band = (lax.axis_index("row") ^ lax.axis_index("col")) & 1
    out[upper_band] = own[...]
    out[1 - upper_band] = by_chip(term_of(mine, straight) + part[...])


def couple(mine, straight, part, own):
    return pl.pallas_call(
        couple_kernel,
        out_shape=jax.ShapeDtypeStruct((2,) + TERMS, BF),
        in_specs=[VM] * 4,
        out_specs=VM,
        compiler_params=vmem(8),
        name="couple",
        cost_estimate=cost(10**9, 6 * 2**20),
    )(mine, straight, part, own)


def both_ways(pairs):
    return pairs + [(j, i) for i, j in pairs]


def local(a_tiles, a_rows, a_cols, a_count, p_panels):
    n_row, n_col = lax.axis_size("row"), lax.axis_size("col")
    row, col = lax.axis_index("row"), lax.axis_index("col")
    even_pairs = both_ways([(i, i + 1) for i in range(0, n_col - 1, 2)])
    odd_pairs = both_ways([(i, i + 1) for i in range(1, n_col - 1, 2)])
    chip = both_ways([(i, i + 1) for i in range(0, n_row - 1, 2)])
    bridges = both_ways([(i, i + 1) for i in range(1, n_row - 1, 2)])
    low_col = (col & 1) == 0
    col_pairs = (even_pairs, odd_pairs)
    straight = lax.ppermute(p_panels, ("row", "col"), [
        (r * n_col + i, r * n_col + j) for r in range(n_row) for i, j in col_pairs[r & 1]
    ])

    def sums(_):
        other = lax.ppermute(p_panels, "row", bridges)
        partner = lax.ppermute(p_panels, "row", chip)
        cross = lax.ppermute(p_panels, ("row", "col"), [
            (r * n_col + i, (r ^ 1) * n_col + j)
            for r in range(n_row)
            for i, j in col_pairs[1 - (r & 1)]
        ])
        codes, counts = plan(a_rows, a_cols, a_count)
        before = first_sums(codes, counts, a_tiles, p_panels, partner)
        mine, theirs, terms = second_sums(codes, counts, a_tiles, other, before, p_panels)
        return mine, partner_term(lax.ppermute(theirs, "row", chip), cross), terms

    def nothing(_):
        return jnp.zeros(TURNED, BF), jnp.zeros((BAND, BAND), F32), jnp.zeros(TERMS, BF)

    mine, part, terms = lax.cond(row < n_row, sums, nothing, 0)
    both = couple(mine, straight, part, terms)
    first_core = (row & 1) == 0
    upper_band = ((row ^ col) & 1) == 1
    groups = [
        [(2 * i + core) * n_col + (c + k) % n_col for k in range(2) for i in range(CHIPS)]
        for core in range(2)
        for c in range(core, n_col, 2)
    ]
    both = both.reshape((2 * CHIPS,) + TERMS[1:])
    both = lax.all_to_all(both, ("row", "col"), 0, 0, axis_index_groups=groups)
    lower, upper = both.reshape((2,) + TERMS).astype(F32).sum(1)
    own = jnp.where(upper_band, upper, lower)
    ends = jnp.where(upper_band, lower, upper)
    mine = jnp.stack([own, ends]).reshape(2, 2, 8, BAND)
    kept = jnp.where(first_core, mine[:, 0], mine[:, 1])
    given = lax.ppermute(jnp.where(first_core, mine[:, 1], mine[:, 0]), "row", chip)
    from_even = jnp.where(first_core, kept[1], given[1])
    from_odd = jnp.where(first_core, given[1], kept[1])
    left = jnp.where(low_col, from_odd, from_even)
    right = jnp.where(low_col, from_even, from_odd)
    return jnp.concatenate([left, kept[0] + given[0], right], axis=1)[None]


def solution(mesh):
    in_specs = (
        P("row", "col", None, None),
        P("row", "col"),
        P("row", "col"),
        P("row", "col"),
        P(("row", "col"), None, None),
    )
    out_specs = P("col", "row", None)
    return jax.shard_map(local, mesh=mesh, in_specs=in_specs, out_specs=out_specs, check_vma=False)
```

```python
import functools

import jax
import jax.numpy as jnp
from jax import lax
from jax.experimental import pallas as pl
from jax.experimental.pallas import tpu as pltpu
from jax.sharding import PartitionSpec as P

BF = jnp.bfloat16
F32 = jnp.float32
PANELS = 16
TILE = 128
BAND = 256
SLOTS = 256
UNROLL = 16
STEP = 8
LIST = SLOTS + UNROLL
SM = pl.BlockSpec(memory_space=pltpu.SMEM)
VM = pl.BlockSpec(memory_space=pltpu.VMEM)
SUMS = (3 * PANELS + 1, TILE, BAND)
CHIPS = 16
TERMS = (CHIPS, 16, BAND)
TURNED = (BAND, PANELS * TILE)


def vmem(mib):
    return pltpu.CompilerParams(vmem_limit_bytes=mib * 2**20)


def cost(flops, nbytes):
    return pl.CostEstimate(flops=flops, bytes_accessed=nbytes, transcendentals=0)


def plan_kernel(rows, cols, count, codes, counts):
    live = count[0, 0]

    def put(step, pos):
        n = list(pos)
        for u in range(STEP):
            t = step * STEP + u
            r, c = rows[0, t], cols[0, t]
            q = c >> 4
            base = jnp.where(q == 0, n[0], jnp.where(q == 1, n[1], n[2]))
            ok = t < live
            codes[jnp.where(ok, base, 3 * LIST)] = t * 1024 + r * 16 + (c & 15)
            n = [n[i] + (ok & (q == i)).astype(jnp.int32) for i in range(3)]
        return tuple(n)

    steps = (live + STEP - 1) // STEP
    ends = lax.fori_loop(0, steps, put, tuple(jnp.int32(i * LIST) for i in range(3)))
    for i in range(3):
        counts[i] = ends[i] - i * LIST
        for u in range(UNROLL):
            codes[ends[i] + u] = 3 * PANELS * 16


def plan(rows, cols, count):
    return pl.pallas_call(
        plan_kernel,
        out_shape=(
            jax.ShapeDtypeStruct((3 * LIST + 1,), jnp.int32),
            jax.ShapeDtypeStruct((3,), jnp.int32),
        ),
        in_specs=[SM] * 3,
        out_specs=(SM, SM),
        compiler_params=vmem(2),
        name="plan",
        cost_estimate=cost(30 * 10**9, 10**4),
    )(rows, cols, count)


def apply_tiles(which, codes, counts, a_tiles, panels, sums):
    def step(g, carry):
        applied, rows = [], []
        for u in range(UNROLL):
            code = codes[which * LIST + g * UNROLL + u]
            rows.append((code >> 4) & 63)
            product = jnp.dot(a_tiles[0, code >> 10], panels[code & 15], preferred_element_type=F32)
            applied.append(product.astype(BF).astype(F32))
        for u in range(UNROLL):
            sums[rows[u]] += applied[u]
        return carry

    lax.fori_loop(0, (counts[which] + UNROLL - 1) // UNROLL, step, 0)


def first_kernel(codes, counts, a_tiles, own, partner, sums):
    def zero(i, carry):
        sums[i] = jnp.zeros((TILE, BAND), F32)
        return carry

    lax.fori_loop(0, 3 * PANELS + 1, zero, 0)
    apply_tiles(1, codes, counts, a_tiles, own, sums)
    apply_tiles(2 - 2 * (lax.axis_index("row") & 1), codes, counts, a_tiles, partner, sums)


def term_of(turned, panels):
    rows = panels[...].reshape(PANELS * TILE, BAND)
    return jnp.dot(turned[...], rows, preferred_element_type=F32)


def by_chip(term):
    return term.T.reshape(TERMS).astype(BF)


def turn(sums, part, ref):
    for k in range(PANELS):
        ref[:, pl.ds(k * TILE, TILE)] = sums[part * PANELS + k].astype(BF).T


def my_offset():
    return 2 * (1 - ((lax.axis_index("col") ^ lax.axis_index("row")) & 1))


def second_kernel(codes, counts, a_tiles, other, before, sums, theirs):
    apply_tiles(2 * (lax.axis_index("row") & 1), codes, counts, a_tiles, other, sums)
    turn(sums, 2 - my_offset(), theirs)


def own_kernel(sums, own, mine, terms, turned):
    turn(sums, my_offset(), mine)
    turn(sums, 1, turned)
    terms[...] = by_chip(term_of(turned, own))


def own_terms(sums, own):
    return pl.pallas_call(
        own_kernel,
        out_shape=(jax.ShapeDtypeStruct(TURNED, BF), jax.ShapeDtypeStruct(TERMS, BF)),
        in_specs=[VM] * 2,
        out_specs=(VM, VM),
        scratch_shapes=[pltpu.VMEM(TURNED, BF)],
        compiler_params=vmem(20),
        name="own_terms",
        cost_estimate=cost(10 * 10**9, 8 * 2**20),
    )(sums, own)


def first_sums(codes, counts, a_tiles, own, partner):
    return pl.pallas_call(
        first_kernel,
        out_shape=jax.ShapeDtypeStruct(SUMS, F32),
        in_specs=[SM] * 2 + [VM] * 3,
        out_specs=VM,
        compiler_params=vmem(20),
        name="first_sums",
        cost_estimate=cost(10 * 10**9, 16 * 2**20),
    )(codes, counts, a_tiles, own, partner)


def second_sums(codes, counts, a_tiles, other, before):
    return pl.pallas_call(
        second_kernel,
        out_shape=(jax.ShapeDtypeStruct(SUMS, F32), jax.ShapeDtypeStruct(TURNED, BF)),
        in_specs=[SM] * 2 + [VM] * 3,
        out_specs=(VM, VM),
        input_output_aliases={4: 0},
        compiler_params=vmem(24),
        name="second_sums",
        cost_estimate=cost(10 * 10**9, 16 * 2**20),
    )(codes, counts, a_tiles, other, before)


def partner_kernel(received, cross, part):
    part[...] = term_of(received, cross)


def partner_term(received, cross):
    return pl.pallas_call(
        partner_kernel,
        out_shape=jax.ShapeDtypeStruct((BAND, BAND), F32),
        in_specs=[VM] * 2,
        out_specs=VM,
        compiler_params=vmem(8),
        name="partner_term",
        cost_estimate=cost(10**9, 6 * 2**20),
    )(received, cross)


def couple_kernel(mine, straight, part, own, out):
    upper_band = (lax.axis_index("row") ^ lax.axis_index("col")) & 1
    out[:, upper_band] = own[...]
    out[:, 1 - upper_band] = by_chip(term_of(mine, straight) + part[...])


def couple(mine, straight, part, own):
    return pl.pallas_call(
        couple_kernel,
        out_shape=jax.ShapeDtypeStruct((CHIPS, 2) + TERMS[1:], BF),
        in_specs=[VM] * 4,
        out_specs=VM,
        compiler_params=vmem(8),
        name="couple",
        cost_estimate=cost(10**9, 6 * 2**20),
    )(mine, straight, part, own)


def both_ways(pairs):
    return pairs + [(j, i) for i, j in pairs]


def local(a_tiles, a_rows, a_cols, a_count, p_panels):
    n_row, n_col = lax.axis_size("row"), lax.axis_size("col")
    row, col = lax.axis_index("row"), lax.axis_index("col")
    even_pairs = both_ways([(i, i + 1) for i in range(0, n_col - 1, 2)])
    odd_pairs = both_ways([(i, i + 1) for i in range(1, n_col - 1, 2)])
    chip = both_ways([(i, i + 1) for i in range(0, n_row - 1, 2)])
    bridges = both_ways([(i, i + 1) for i in range(1, n_row - 1, 2)])
    low_col = (col & 1) == 0
    col_pairs = (even_pairs, odd_pairs)
    straight = lax.ppermute(p_panels, ("row", "col"), [
        (r * n_col + i, r * n_col + j) for r in range(n_row) for i, j in col_pairs[r & 1]
    ])

    def sums(_):
        other = lax.ppermute(p_panels, "row", bridges)
        partner = lax.ppermute(p_panels, "row", chip)
        cross = lax.ppermute(p_panels, ("row", "col"), [
            (r * n_col + i, (r ^ 1) * n_col + j)
            for r in range(n_row)
            for i, j in col_pairs[1 - (r & 1)]
        ])
        codes, counts = plan(a_rows, a_cols, a_count)
        before = first_sums(codes, counts, a_tiles, p_panels, partner)
        after, theirs = second_sums(codes, counts, a_tiles, other, before)
        received = lax.ppermute(theirs, "row", chip)
        mine, terms = own_terms(after, p_panels)
        return mine, partner_term(received, cross), terms

    def nothing(_):
        return jnp.zeros(TURNED, BF), jnp.zeros((BAND, BAND), F32), jnp.zeros(TERMS, BF)

    mine, part, terms = lax.cond(row < n_row, sums, nothing, 0)
    both = couple(mine, straight, part, terms)
    first_core = (row & 1) == 0
    upper_band = ((row ^ col) & 1) == 1
    groups = [
        [(2 * i + core) * n_col + (c + k) % n_col for i in range(CHIPS) for k in range(2)]
        for core in range(2)
        for c in range(core, n_col, 2)
    ]
    both = both.reshape((2 * CHIPS,) + TERMS[1:])
    both = lax.all_to_all(both, ("row", "col"), 0, 0, axis_index_groups=groups)
    lower, upper = both.reshape((CHIPS, 2) + TERMS[1:]).astype(F32).sum(0)
    own = jnp.where(upper_band, upper, lower)
    ends = jnp.where(upper_band, lower, upper)
    mine = jnp.stack([own, ends]).reshape(2, 2, 8, BAND)
    kept = jnp.where(first_core, mine[:, 0], mine[:, 1])
    given = lax.ppermute(jnp.where(first_core, mine[:, 1], mine[:, 0]), "row", chip)
    from_even = jnp.where(first_core, kept[1], given[1])
    from_odd = jnp.where(first_core, given[1], kept[1])
    left = jnp.where(low_col, from_odd, from_even)
    right = jnp.where(low_col, from_even, from_odd)
    return jnp.concatenate([left, kept[0] + given[0], right], axis=1)[None]


def solution(mesh):
    in_specs = (
        P("row", "col", None, None),
        P("row", "col"),
        P("row", "col"),
        P("row", "col"),
        P(("row", "col"), None, None),
    )
    out_specs = P("col", "row", None)
    return jax.shard_map(local, mesh=mesh, in_specs=in_specs, out_specs=out_specs, check_vma=False)
```

```python
import functools

import jax
import jax.numpy as jnp
from jax import lax
from jax.experimental import pallas as pl
from jax.experimental.pallas import tpu as pltpu
from jax.sharding import PartitionSpec as P

BF = jnp.bfloat16
F32 = jnp.float32
PANELS = 16
TILE = 128
BAND = 256
SLOTS = 256
UNROLL = 16
STEP = 8
LIST = SLOTS + UNROLL
SM = pl.BlockSpec(memory_space=pltpu.SMEM)
VM = pl.BlockSpec(memory_space=pltpu.VMEM)
SUMS = (3 * PANELS + 1, TILE, BAND)
CHIPS = 16
TERMS = (CHIPS, 16, BAND)
TURNED = (BAND, PANELS * TILE)


def vmem(mib):
    return pltpu.CompilerParams(vmem_limit_bytes=mib * 2**20)


def cost(flops, nbytes):
    return pl.CostEstimate(flops=flops, bytes_accessed=nbytes, transcendentals=0)


def plan_kernel(rows, cols, count, codes, counts):
    live = count[0, 0]

    def put(step, pos):
        n = list(pos)
        for u in range(STEP):
            t = step * STEP + u
            r, c = rows[0, t], cols[0, t]
            q = c >> 4
            base = jnp.where(q == 0, n[0], jnp.where(q == 1, n[1], n[2]))
            ok = t < live
            codes[jnp.where(ok, base, 3 * LIST)] = t * 1024 + r * 16 + (c & 15)
            n = [n[i] + (ok & (q == i)).astype(jnp.int32) for i in range(3)]
        return tuple(n)

    steps = (live + STEP - 1) // STEP
    ends = lax.fori_loop(0, steps, put, tuple(jnp.int32(i * LIST) for i in range(3)))
    for i in range(3):
        counts[i] = ends[i] - i * LIST
        for u in range(UNROLL):
            codes[ends[i] + u] = 3 * PANELS * 16


def plan(rows, cols, count):
    return pl.pallas_call(
        plan_kernel,
        out_shape=(
            jax.ShapeDtypeStruct((3 * LIST + 1,), jnp.int32),
            jax.ShapeDtypeStruct((3,), jnp.int32),
        ),
        in_specs=[SM] * 3,
        out_specs=(SM, SM),
        compiler_params=vmem(2),
        name="plan",
        cost_estimate=cost(30 * 10**9, 10**4),
    )(rows, cols, count)


def apply_tiles(which, codes, counts, a_tiles, panels, sums):
    def step(g, carry):
        applied, rows = [], []
        for u in range(UNROLL):
            code = codes[which * LIST + g * UNROLL + u]
            rows.append((code >> 4) & 63)
            product = jnp.dot(a_tiles[0, code >> 10], panels[code & 15], preferred_element_type=F32)
            applied.append(product.astype(BF).astype(F32))
        for u in range(UNROLL):
            sums[rows[u]] += applied[u]
        return carry

    lax.fori_loop(0, (counts[which] + UNROLL - 1) // UNROLL, step, 0)


def first_kernel(codes, counts, a_tiles, own, partner, sums):
    def zero(i, carry):
        sums[i] = jnp.zeros((TILE, BAND), F32)
        return carry

    lax.fori_loop(0, 3 * PANELS + 1, zero, 0)
    apply_tiles(1, codes, counts, a_tiles, own, sums)
    apply_tiles(2 - 2 * (lax.axis_index("row") & 1), codes, counts, a_tiles, partner, sums)


def term_of(turned, panels):
    rows = panels[...].reshape(PANELS * TILE, BAND)
    return jnp.dot(turned[...], rows, preferred_element_type=F32)


def by_chip(term):
    return term.T.reshape(TERMS).astype(BF)


def turn(sums, part, ref):
    for k in range(PANELS):
        ref[:, pl.ds(k * TILE, TILE)] = sums[part * PANELS + k].astype(BF).T


def my_offset():
    return 2 * (1 - ((lax.axis_index("col") ^ lax.axis_index("row")) & 1))


def second_kernel(codes, counts, a_tiles, other, before, sums, theirs):
    apply_tiles(2 * (lax.axis_index("row") & 1), codes, counts, a_tiles, other, sums)
    turn(sums, 2 - my_offset(), theirs)


def own_kernel(sums, own, mine, terms, turned):
    turn(sums, my_offset(), mine)
    turn(sums, 1, turned)
    terms[...] = by_chip(term_of(turned, own))


def own_terms(sums, own):
    return pl.pallas_call(
        own_kernel,
        out_shape=(jax.ShapeDtypeStruct(TURNED, BF), jax.ShapeDtypeStruct(TERMS, BF)),
        in_specs=[VM] * 2,
        out_specs=(VM, VM),
        scratch_shapes=[pltpu.VMEM(TURNED, BF)],
        compiler_params=vmem(20),
        name="own_terms",
        cost_estimate=cost(10 * 10**9, 8 * 2**20),
    )(sums, own)


def first_sums(codes, counts, a_tiles, own, partner):
    return pl.pallas_call(
        first_kernel,
        out_shape=jax.ShapeDtypeStruct(SUMS, F32),
        in_specs=[SM] * 2 + [VM] * 3,
        out_specs=VM,
        compiler_params=vmem(20),
        name="first_sums",
        cost_estimate=cost(10 * 10**9, 16 * 2**20),
    )(codes, counts, a_tiles, own, partner)


def second_sums(codes, counts, a_tiles, other, before):
    return pl.pallas_call(
        second_kernel,
        out_shape=(jax.ShapeDtypeStruct(SUMS, F32), jax.ShapeDtypeStruct(TURNED, BF)),
        in_specs=[SM] * 2 + [VM] * 3,
        out_specs=(VM, VM),
        input_output_aliases={4: 0},
        compiler_params=vmem(24),
        name="second_sums",
        cost_estimate=cost(10 * 10**9, 16 * 2**20),
    )(codes, counts, a_tiles, other, before)


def partner_kernel(received, cross, part):
    part[...] = term_of(received, cross)


def partner_term(received, cross):
    return pl.pallas_call(
        partner_kernel,
        out_shape=jax.ShapeDtypeStruct((BAND, BAND), F32),
        in_specs=[VM] * 2,
        out_specs=VM,
        compiler_params=vmem(8),
        name="partner_term",
        cost_estimate=cost(10**9, 6 * 2**20),
    )(received, cross)


def couple_kernel(mine, straight, part, own, out):
    upper_band = (lax.axis_index("row") ^ lax.axis_index("col")) & 1
    out[:, upper_band] = own[...]
    out[:, 1 - upper_band] = by_chip(term_of(mine, straight) + part[...])


def couple(mine, straight, part, own):
    return pl.pallas_call(
        couple_kernel,
        out_shape=jax.ShapeDtypeStruct((CHIPS, 2) + TERMS[1:], BF),
        in_specs=[VM] * 4,
        out_specs=VM,
        compiler_params=vmem(8),
        name="couple",
        cost_estimate=cost(10**9, 6 * 2**20),
    )(mine, straight, part, own)


def fold_kernel(both, kept, given):
    core = lax.axis_index("row") & 1
    upper_band = core ^ (lax.axis_index("col") & 1)
    for at, band in ((0, upper_band), (1, 1 - upper_band)):
        total = both[0, band].astype(F32)
        for i in range(1, CHIPS):
            total = total + both[i, band].astype(F32)
        first = core == 0
        kept[at] = jnp.where(first, total[:8], total[8:])
        given[at] = jnp.where(first, total[8:], total[:8])


def fold(both):
    half = jax.ShapeDtypeStruct((2, 8, BAND), F32)
    return pl.pallas_call(
        fold_kernel,
        out_shape=(half, half),
        in_specs=[VM],
        out_specs=(VM, VM),
        compiler_params=vmem(4),
        name="fold",
        cost_estimate=cost(10**5, 10**5),
    )(both)


def finish_kernel(kept, given, out):
    core, col = lax.axis_index("row") & 1, lax.axis_index("col") & 1
    kept_is_upper = core == col
    out[:, :BAND] = jnp.where(kept_is_upper, given[1], kept[1])
    out[:, BAND:2 * BAND] = kept[0] + given[0]
    out[:, 2 * BAND:] = jnp.where(kept_is_upper, kept[1], given[1])


def finish(kept, given):
    return pl.pallas_call(
        finish_kernel,
        out_shape=jax.ShapeDtypeStruct((8, 3 * BAND), F32),
        in_specs=[VM, VM],
        out_specs=VM,
        compiler_params=vmem(4),
        name="finish",
        cost_estimate=cost(10**4, 10**5),
    )(kept, given)


def both_ways(pairs):
    return pairs + [(j, i) for i, j in pairs]


def local(a_tiles, a_rows, a_cols, a_count, p_panels):
    n_row, n_col = lax.axis_size("row"), lax.axis_size("col")
    row = lax.axis_index("row")
    even_pairs = both_ways([(i, i + 1) for i in range(0, n_col - 1, 2)])
    odd_pairs = both_ways([(i, i + 1) for i in range(1, n_col - 1, 2)])
    chip = both_ways([(i, i + 1) for i in range(0, n_row - 1, 2)])
    bridges = both_ways([(i, i + 1) for i in range(1, n_row - 1, 2)])
    col_pairs = (even_pairs, odd_pairs)
    straight = lax.ppermute(p_panels, ("row", "col"), [
        (r * n_col + i, r * n_col + j) for r in range(n_row) for i, j in col_pairs[r & 1]
    ])

    def sums(_):
        other = lax.ppermute(p_panels, "row", bridges)
        partner = lax.ppermute(p_panels, "row", chip)
        cross = lax.ppermute(p_panels, ("row", "col"), [
            (r * n_col + i, (r ^ 1) * n_col + j)
            for r in range(n_row)
            for i, j in col_pairs[1 - (r & 1)]
        ])
        codes, counts = plan(a_rows, a_cols, a_count)
        before = first_sums(codes, counts, a_tiles, p_panels, partner)
        after, theirs = second_sums(codes, counts, a_tiles, other, before)
        received = lax.ppermute(theirs, "row", chip)
        mine, terms = own_terms(after, p_panels)
        return mine, partner_term(received, cross), terms

    def nothing(_):
        return jnp.zeros(TURNED, BF), jnp.zeros((BAND, BAND), F32), jnp.zeros(TERMS, BF)

    mine, part, terms = lax.cond(row < n_row, sums, nothing, 0)
    both = couple(mine, straight, part, terms)
    groups = [
        [(2 * i + core) * n_col + (c + k) % n_col for i in range(CHIPS) for k in range(2)]
        for core in range(2)
        for c in range(core, n_col, 2)
    ]
    both = both.reshape((2 * CHIPS,) + TERMS[1:])
    both = lax.all_to_all(both, ("row", "col"), 0, 0, axis_index_groups=groups)
    mine, given = fold(both.reshape((CHIPS, 2) + TERMS[1:]))
    return finish(mine, lax.ppermute(given, "row", chip))[None]


def solution(mesh):
    in_specs = (
        P("row", "col", None, None),
        P("row", "col"),
        P("row", "col"),
        P("row", "col"),
        P(("row", "col"), None, None),
    )
    out_specs = P("col", "row", None)
    return jax.shard_map(local, mesh=mesh, in_specs=in_specs, out_specs=out_specs, check_vma=False)
```
